32 devices in a mesh: grp: 2 (over y), tile: 16 (over z, x, core).
Axes of the slice: x: 2, y: 2, z: 4, core: 2. Of those that a mesh axis runs over, the one named last changes fastest.
Arguments:
- sensitivity: bfloat16 [4, 2048, 3, 1024], P('grp', 'tile'), may hold values from -6 to 6
- inst_weight: float32 [4], P('grp'), may hold values from 0.3 to 3
- filter_taps: bfloat16 [129], replicated, may hold values from 0.019897461 to 0.13964844
- basis_rows: bfloat16 [128, 16], replicated, may hold values from -0.5 to 0.5
- basis_cols: bfloat16 [128, 16], replicated, may hold values from -0.5 to 0.5
- box_table: int32 [128, 1], replicated, may hold values from 0 to 31
- owner_perm: int32 [32], replicated, may hold values from 0 to 31, each once
Outputs:
- design_grad: float32 [32, 3, 256], P(('grp', 'tile'))
The draws below stay inside these ranges and needn't reach their ends.
Inputs may be any that keep to these rules, and one draw needn't show every extreme that they name: `box_table`: every one of the 32 boxes is named by at least one tile. `owner_perm`: each box appears exactly once.
All inputs are finite; a program needn't handle non-finite values.
Results may differ from the reference program's by a relative error of at most 0.017.
Values may be sent and summed in bfloat16 or wider, within the bound.
A program may use at most 64 MiB of HBM per device.

```python
import math
import jax
import jax.numpy as jnp
from jax import lax

G2 = 1024
INST_GRP = 2
TAPS = 129
TR = 128
TC = 128
KR = 16
KC = 16
G1 = 2048
INSTANCES = 4
NB = 32
NTILES = 128


def block_scale(key, dims, pieces, low, top_value):
    loudness = 1.0
    for dim, shards_of in pieces:
        steps = jax.random.uniform(jax.random.fold_in(jax.random.fold_in(key, 6), dim), (shards_of,), jnp.float32, low / len(pieces), top_value / len(pieces))
        loudness = loudness * jnp.repeat(jnp.exp(steps), dims[dim] // shards_of).reshape((-1,) + (1,) * (len(dims) - 1 - dim))
    return loudness


def distinct(key, rows, count, top, lift):
    sequence = jax.random.permutation(jax.random.fold_in(key, 1), count)
    boost = sequence
    for power in range(3):
        boost = boost * boost // count
    boost = boost * lift // count
    lots = jax.random.randint(jax.random.fold_in(key, 2), (rows, count), 0, 4096) + boost
    sure = jax.random.permutation(jax.random.fold_in(key, 3), rows)[jnp.arange(count) % rows]
    lots = jnp.where(jnp.arange(rows)[:, None] == sure[None, :], 1 << 14, lots)
    merit = lots * count + jnp.arange(count)
    return lax.top_k(merit.astype(jnp.int32), top)[1].astype(jnp.int32)


def scatter_about(own_key, shape, deviation, limit, shards=(), kind=jnp.bfloat16):
    level = block_scale(own_key, shape, shards, -0.22, 0.18) if shards else 1.0
    entries = jax.random.normal(own_key, shape, jnp.float32) * deviation * level
    return jnp.minimum(jnp.maximum(entries, -limit), limit).astype(kind)


def setup_inputs(seed: int = 0) -> dict:
    seeds = jax.random.split(jax.random.key(seed), 8)
    return {
        "sensitivity": scatter_about(seeds[0], (INSTANCES, G1, 3, G2), 1.0, 6.0, ((0, 2), (1, 16))),
        "inst_weight": jnp.clip(jnp.exp(math.log(3.0) - 2.3025851 * jax.random.uniform(seeds[1], (INSTANCES,), jnp.float32) ** block_scale(seeds[1], (INSTANCES,), ((0, 2),), -0.2, 0.2)), 0.3, 3.0),
        "filter_taps": jnp.clip(jax.random.uniform(seeds[2], (TAPS,), jnp.float32, 0.019897461, 0.13964844), 0.019897461, 0.13964844).astype(jnp.bfloat16),
        "basis_rows": scatter_about(seeds[3], (TR, KR), TR ** -0.5, 0.5),
        "basis_cols": scatter_about(seeds[4], (TC, KC), TC ** -0.5, 0.5),
        "box_table": distinct(seeds[5], NTILES, NB, 1, 0),
        "owner_perm": jax.random.permutation(seeds[6], NB).astype(jnp.int32),
    }


def smooth_axis(field, filter_taps, axis):
    reach = filter_taps.shape[0] - 1
    half = reach // 2
    length = field.shape[axis]
    widths = [(0, 0)] * field.ndim
    widths[axis] = (half, half)
    padded = jnp.pad(field.astype(jnp.float32), widths)
    weights = filter_taps.astype(jnp.float32)
    total = jnp.zeros(field.shape, jnp.float32)
    for offset in range(reach + 1):
        total = total + weights[offset] * lax.slice_in_dim(padded, offset, offset + length, axis=axis)
    return total.astype(jnp.bfloat16)


def reference(sensitivity, inst_weight, filter_taps, basis_rows, basis_cols, box_table, owner_perm):
    rows_all = sensitivity.shape[1]
    cols_all = sensitivity.shape[3]
    groups = sensitivity.shape[0] // INST_GRP
    boxes = owner_perm.shape[0]
    grouped = sensitivity.reshape(groups, INST_GRP, rows_all, 3, cols_all)
    weights = inst_weight.reshape(groups, INST_GRP)

    def one_group(pair):
        block, weight = pair
        summed = jnp.sum(block.astype(jnp.float32) * weight[:, None, None, None], axis=0).astype(jnp.bfloat16)
        first = smooth_axis(summed, filter_taps, 2)
        second = smooth_axis(first, filter_taps, 0)
        tiles = second.reshape(rows_all // TR, TR, 3, cols_all // TC, TC).astype(jnp.float32)
        rowwise = jnp.einsum("xakyc,ap->xykpc", tiles, basis_rows.astype(jnp.float32), precision=lax.Precision.HIGHEST)
        tile_part = jnp.einsum("xykpc,cq->xykpq", rowwise, basis_cols.astype(jnp.float32), precision=lax.Precision.HIGHEST)
        flat = tile_part.reshape(-1, 3 * KR * KC)
        return jax.ops.segment_sum(flat, box_table[:, 0], num_segments=boxes)

    box_grad = jnp.sum(lax.map(one_group, (grouped, weights)), axis=0)
    return box_grad[owner_perm].reshape(boxes, 3, KR * KC)
```

```python
import functools

import jax
import jax.numpy as jnp
from jax import lax
from jax.experimental import pallas as pl
from jax.experimental.pallas import tpu as pltpu
from jax.sharding import PartitionSpec as P

MESH = pl.DeviceIdType.MESH
F32 = jnp.float32
BF16 = jnp.bfloat16
LANES = 128


def iota(shape, dim):
    return lax.broadcasted_iota(jnp.int32, shape, dim)


def dot(a, b):
    return jnp.dot(a, b, preferred_element_type=F32)


def kernel(
    dims, sens_hbm, weight, taps_ref, rows_ref, cols_ref, table_ref, owner_ref, out_ref,
    sens, taps_wide, col_op, msg, recv, load_sem, send_sem, recv_sem,
):
    grps, tiles = dims
    devices = grps * tiles
    insts, comps, height, width = sens.shape
    ctrl, tile = rows_ref.shape
    tile_cols = width // tile
    half = (taps_ref.shape[1] - 1) // 2
    wide = 3 * tile
    low = LANES // ctrl
    high = ctrl // low
    slots = owner_ref.shape[1]
    ntiles = table_ref.shape[1]
    tile_pos = lax.axis_index("tile")
    me = lax.axis_index("grp") * tiles + tile_pos

    load = pltpu.make_async_copy(sens_hbm, sens, load_sem)
    load.start()

    barrier = pltpu.get_barrier_semaphore()

    def greet(step, carry):
        to = lax.rem(me + step, devices)
        pl.semaphore_signal(
            barrier, inc=1, device_id=(to // tiles, lax.rem(to, tiles)), device_id_type=MESH
        )
        return carry

    lax.fori_loop(1, devices, greet, 0)

    taps_wide[...] = jnp.zeros_like(taps_wide)
    taps_wide[:, : taps_ref.shape[1]] = taps_ref[...].astype(F32)
    spread = jnp.broadcast_to(taps_wide[...], (tile, wide))
    band = pltpu.roll(spread, tile - half, 1, stride=1, stride_axis=0).astype(BF16)
    row_op = dot(rows_ref[...], band).astype(BF16)
    piece = dot(cols_ref[...], band).astype(BF16)
    col_op[...] = jnp.zeros_like(col_op)
    for y in range(tile_cols):
        first = max(y - 1, 0)
        last = min(y + 2, tile_cols)
        col_op[y * ctrl : (y + 1) * ctrl, first * tile : last * tile] = piece[
            :, (first - y + 1) * tile : (last - y + 1) * tile
        ]
    row_ops = jnp.concatenate(
        [row_op[:, d * tile : (d + 1) * tile] for d in (2, 1, 0)], axis=0
    )

    owner_wide = jnp.broadcast_to(owner_ref[...].astype(F32), (slots, slots))
    owner = jnp.sum(
        jnp.where(iota((slots, slots), 0) == iota((slots, slots), 1), owner_wide, 0.0),
        axis=1, keepdims=True,
    )
    hit = jnp.where(owner == table_ref[...].astype(F32), 1.0, 0.0).astype(BF16)
    span = tile_cols * 3 * low
    lane = iota((ntiles, span), 1)
    y_of = lane // (3 * low)
    x_of = lax.rem(lane // low, 3) + tile_pos - 1
    wanted = (iota((ntiles, span), 0) == x_of * tile_cols + y_of) & (x_of >= 0) & (x_of < tiles)
    select = dot(hit, jnp.where(wanted, 1.0, 0.0).astype(BF16)).astype(BF16)

    copies = tile_cols * LANES
    from_row = iota((LANES, copies), 0)
    to_lane = iota((LANES, copies), 1)
    expand = jnp.where(
        (from_row // ctrl == to_lane // LANES) & (lax.rem(from_row, ctrl) == lax.rem(to_lane, ctrl)),
        1.0, 0.0,
    ).astype(BF16)
    keep = iota((low, LANES), 0) == iota((low, LANES), 1) // ctrl

    load.wait()
    field = sens[...].reshape(insts * comps * height, width)
    smooth = lax.dot_general(
        field, col_op[...], (((1,), (1,)), ((), ())), preferred_element_type=F32
    )
    block = comps * height
    total = weight[0] * smooth[:block]
    for i in range(1, insts):
        total = total + weight[i] * smooth[i * block : (i + 1) * block]
    total = total.astype(BF16)
    parts = jnp.concatenate(
        [dot(row_ops, total[k * height : (k + 1) * height]) for k in range(comps)], axis=0
    ).astype(BF16)
    grown = dot(parts, expand)
    columns = []
    for k in range(comps):
        for h in range(high):
            pieces = []
            for y in range(tile_cols):
                for d in range(3):
                    at = (k * 3 + d) * ctrl + h * low
                    pieces.append(
                        jnp.where(keep, grown[at : at + low, y * LANES : (y + 1) * LANES], 0.0)
                    )
            columns.append(jnp.concatenate(pieces, axis=0))
    stacked = jnp.concatenate(columns, axis=1).astype(BF16)
    boxes = dot(select, stacked)
    for j in range(comps * high):
        msg[:, j, :] = boxes[:, j * LANES : (j + 1) * LANES]

    pl.semaphore_wait(barrier, devices - 1)

    def push(step, carry):
        to = lax.rem(me + step, devices)
        pltpu.make_async_remote_copy(
            src_ref=msg.at[to],
            dst_ref=recv.at[step - 1],
            send_sem=send_sem,
            recv_sem=recv_sem,
            device_id=(to // tiles, lax.rem(to, tiles)),
            device_id_type=MESH,
        ).start()
        return carry

    lax.fori_loop(1, devices, push, 0)
    pltpu.make_async_copy(recv, recv, recv_sem).wait()
    result = msg[me] + jnp.sum(recv[...], axis=0)
    for k in range(comps):
        for h in range(high):
            j = k * high + h
            out_ref[0, k : k + 1, h * LANES : (h + 1) * LANES] = result[j : j + 1]
    pltpu.make_async_copy(recv, recv, send_sem).wait()


def solution(mesh):
    grps, tiles = mesh.shape["grp"], mesh.shape["tile"]
    devices = grps * tiles

    def local(sens, weight, taps, rows, cols, table, owner):
        field = sens.transpose(0, 2, 1, 3)
        insts, comps, height, width = field.shape
        tile, ctrl = rows.shape
        slots = owner.shape[0]
        assert height == tile and slots == devices and LANES % ctrl == 0
        assert width // tile * ctrl == LANES and ctrl * ctrl % LANES == 0
        vmem = pl.BlockSpec(memory_space=pltpu.VMEM)
        lines = comps * ctrl * ctrl // LANES
        return pl.pallas_call(
            functools.partial(kernel, (grps, tiles)),
            out_shape=jax.ShapeDtypeStruct((1, comps, ctrl * ctrl), F32),
            in_specs=[
                pl.BlockSpec(memory_space=pl.ANY),
                pl.BlockSpec(memory_space=pltpu.SMEM),
                vmem, vmem, vmem, vmem, vmem,
            ],
            out_specs=vmem,
            scratch_shapes=[
                pltpu.VMEM((insts, comps, height, width), BF16),
                pltpu.VMEM((1, 3 * tile), F32),
                pltpu.VMEM((LANES, width), BF16),
                pltpu.VMEM((slots, lines, LANES), F32),
                pltpu.VMEM((devices - 1, lines, LANES), F32),
                pltpu.SemaphoreType.DMA,
                pltpu.SemaphoreType.DMA,
                pltpu.SemaphoreType.DMA,
            ],
            compiler_params=pltpu.CompilerParams(
                collective_id=0, has_side_effects=True, vmem_limit_bytes=32 * 1024 * 1024
            ),
        )(
            field, weight, taps.reshape(1, -1), rows.T, cols.T,
            table.reshape(1, -1), owner.reshape(1, -1),
        )

    placed = (P("grp", "tile", None, None), P("grp"), P(), P(), P(), P(), P())
    return jax.shard_map(
        local, mesh=mesh, in_specs=placed, out_specs=P(("grp", "tile"), None, None), check_vma=False
    )
```

```python
import functools

import jax
import jax.numpy as jnp
from jax import lax
from jax.experimental import pallas as pl
from jax.experimental.pallas import tpu as pltpu
from jax.sharding import PartitionSpec as P

MESH = pl.DeviceIdType.MESH
F32 = jnp.float32
BF16 = jnp.bfloat16
LANES = 128


def iota(shape, dim):
    return lax.broadcasted_iota(jnp.int32, shape, dim)


def dot(a, b):
    return jnp.dot(a, b, preferred_element_type=F32)


def kernel(
    dims, sens_hbm, weight_hbm, taps_hbm, rows_hbm, cols_hbm, table_hbm, owner_hbm, out_ref,
    sens, weight, taps_ref, rows_ref, cols_ref, table_ref, owner_ref,
    taps_wide, col_op, msg, recv, load_sems, send_sem, recv_sem,
):
    grps, tiles = dims
    devices = grps * tiles
    insts, comps, height, width = sens.shape
    ctrl, tile = rows_ref.shape
    tile_cols = width // tile
    half = (taps_ref.shape[0] - 1) // 2
    wide = 3 * tile
    low = LANES // ctrl
    high = ctrl // low
    slots = owner_ref.shape[1]
    ntiles = table_ref.shape[1]
    tile_pos = lax.axis_index("tile")
    me = lax.axis_index("grp") * tiles + tile_pos

    loads = [
        pltpu.make_async_copy(source, held, load_sems.at[n])
        for n, (source, held) in enumerate((
            (taps_hbm, taps_ref), (rows_hbm, rows_ref), (cols_hbm, cols_ref),
            (owner_hbm, owner_ref), (table_hbm, table_ref), (weight_hbm, weight),
            (sens_hbm, sens),
        ))
    ]
    for load in loads:
        load.start()

    barrier = pltpu.get_barrier_semaphore()

    def greet(step, carry):
        to = lax.rem(me + step, devices)
        pl.semaphore_signal(
            barrier, inc=1, device_id=(to // tiles, lax.rem(to, tiles)), device_id_type=MESH
        )
        return carry

    lax.fori_loop(1, devices, greet, 0)

    taps_wide[...] = jnp.zeros_like(taps_wide)
    for load in loads[:-1]:
        load.wait()
    taps_wide[:, : taps_ref.shape[0]] = taps_ref[...].astype(F32).reshape(1, -1)
    spread = jnp.broadcast_to(taps_wide[...], (tile, wide))
    band = pltpu.roll(spread, tile - half, 1, stride=1, stride_axis=0).astype(BF16)
    row_op = dot(rows_ref[...], band).astype(BF16)
    piece = dot(cols_ref[...], band).astype(BF16)
    col_op[...] = jnp.zeros_like(col_op)
    for y in range(tile_cols):
        first = max(y - 1, 0)
        last = min(y + 2, tile_cols)
        col_op[y * ctrl : (y + 1) * ctrl, first * tile : last * tile] = piece[
            :, (first - y + 1) * tile : (last - y + 1) * tile
        ]
    row_ops = jnp.concatenate(
        [row_op[:, d * tile : (d + 1) * tile] for d in (2, 1, 0)], axis=0
    )

    owner_wide = jnp.broadcast_to(owner_ref[...].astype(F32), (slots, slots))
    owner = jnp.sum(
        jnp.where(iota((slots, slots), 0) == iota((slots, slots), 1), owner_wide, 0.0),
        axis=1, keepdims=True,
    )
    hit = jnp.where(owner == table_ref[...].astype(F32), 1.0, 0.0).astype(BF16)
    span = tile_cols * 3 * low
    lane = iota((ntiles, span), 1)
    y_of = lane // (3 * low)
    x_of = lax.rem(lane // low, 3) + tile_pos - 1
    wanted = (iota((ntiles, span), 0) == x_of * tile_cols + y_of) & (x_of >= 0) & (x_of < tiles)
    select = dot(hit, jnp.where(wanted, 1.0, 0.0).astype(BF16)).astype(BF16)

    copies = tile_cols * LANES
    from_row = iota((LANES, copies), 0)
    to_lane = iota((LANES, copies), 1)
    expand = jnp.where(
        (from_row // ctrl == to_lane // LANES) & (lax.rem(from_row, ctrl) == lax.rem(to_lane, ctrl)),
        1.0, 0.0,
    ).astype(BF16)
    keep = iota((low, LANES), 0) == iota((low, LANES), 1) // ctrl

    loads[-1].wait()
    field = sens[...].reshape(insts * comps * height, width)
    smooth = lax.dot_general(
        field, col_op[...], (((1,), (1,)), ((), ())), preferred_element_type=F32
    )
    block = comps * height
    total = weight[0] * smooth[:block]
    for i in range(1, insts):
        total = total + weight[i] * smooth[i * block : (i + 1) * block]
    total = total.astype(BF16)
    parts = jnp.concatenate(
        [dot(row_ops, total[k * height : (k + 1) * height]) for k in range(comps)], axis=0
    ).astype(BF16)
    grown = dot(parts, expand)
    columns = []
    for k in range(comps):
        for h in range(high):
            pieces = []
            for y in range(tile_cols):
                for d in range(3):
                    at = (k * 3 + d) * ctrl + h * low
                    pieces.append(
                        jnp.where(keep, grown[at : at + low, y * LANES : (y + 1) * LANES], 0.0)
                    )
            columns.append(jnp.concatenate(pieces, axis=0))
    stacked = jnp.concatenate(columns, axis=1).astype(BF16)
    boxes = dot(select, stacked)
    for j in range(comps * high):
        msg[:, j, :] = boxes[:, j * LANES : (j + 1) * LANES]

    pl.semaphore_wait(barrier, devices - 1)

    def push(step, carry):
        to = lax.rem(me + step, devices)
        pltpu.make_async_remote_copy(
            src_ref=msg.at[to],
            dst_ref=recv.at[step - 1],
            send_sem=send_sem,
            recv_sem=recv_sem,
            device_id=(to // tiles, lax.rem(to, tiles)),
            device_id_type=MESH,
        ).start()
        return carry

    lax.fori_loop(1, devices, push, 0)
    pltpu.make_async_copy(recv, recv, recv_sem).wait()
    result = msg[me] + jnp.sum(recv[...], axis=0)
    for k in range(comps):
        for h in range(high):
            j = k * high + h
            out_ref[k, :, h * LANES : (h + 1) * LANES] = result[j : j + 1]
    pltpu.make_async_copy(recv, recv, send_sem).wait()


def solution(mesh):
    grps, tiles = mesh.shape["grp"], mesh.shape["tile"]
    devices = grps * tiles

    def local(sens, weight, taps, rows, cols, table, owner):
        field = sens.transpose(0, 2, 1, 3)
        insts, comps, height, width = field.shape
        tile, ctrl = rows.shape
        slots = owner.shape[0]
        assert height == tile and slots == devices and LANES % ctrl == 0
        assert width // tile * ctrl == LANES and ctrl * ctrl % LANES == 0
        lines = comps * ctrl * ctrl // LANES
        return pl.pallas_call(
            functools.partial(kernel, (grps, tiles)),
            out_shape=jax.ShapeDtypeStruct((comps, 1, ctrl * ctrl), F32),
            in_specs=[pl.BlockSpec(memory_space=pltpu.HBM)] * 7,
            out_specs=pl.BlockSpec(memory_space=pltpu.VMEM),
            scratch_shapes=[
                pltpu.VMEM((insts, comps, height, width), BF16),
                pltpu.SMEM(weight.shape, F32),
                pltpu.VMEM(taps.shape, BF16),
                pltpu.VMEM((ctrl, tile), BF16),
                pltpu.VMEM((ctrl, tile), BF16),
                pltpu.VMEM((1, table.shape[0]), jnp.int32),
                pltpu.VMEM((1, slots), jnp.int32),
                pltpu.VMEM((1, 3 * tile), F32),
                pltpu.VMEM((LANES, width), BF16),
                pltpu.VMEM((slots, lines, LANES), F32),
                pltpu.VMEM((devices - 1, lines, LANES), F32),
                pltpu.SemaphoreType.DMA((7,)),
                pltpu.SemaphoreType.DMA,
                pltpu.SemaphoreType.DMA,
            ],
            compiler_params=pltpu.CompilerParams(
                collective_id=0, has_side_effects=True
            ),
        )(
            field, weight, taps, rows.T, cols.T, table.reshape(1, -1), owner.reshape(1, -1)
        ).transpose(1, 0, 2)

    placed = (P("grp", "tile", None, None), P("grp"), P(), P(), P(), P(), P())
    return jax.shard_map(
        local, mesh=mesh, in_specs=placed, out_specs=P(("grp", "tile"), None, None), check_vma=False
    )
```

```python
import functools

import jax
import jax.numpy as jnp
from jax import lax
from jax.experimental import pallas as pl
from jax.experimental.pallas import tpu as pltpu
from jax.sharding import PartitionSpec as P

MESH = pl.DeviceIdType.MESH
F32 = jnp.float32
BF16 = jnp.bfloat16
LANES = 128


def iota(shape, dim):
    return lax.broadcasted_iota(jnp.int32, shape, dim)


def dot(a, b):
    return jnp.dot(a, b, preferred_element_type=F32)


def kernel(
    dims, sens_hbm, weight_hbm, taps_hbm, rows_hbm, cols_hbm, table_hbm, owner_hbm, out_ref,
    sens, weight, taps_ref, rows_ref, cols_ref, table_ref, owner_ref,
    taps_wide, col_op, wanted_ref, expand_ref, msg, recv, load_sems, send_sem, recv_sem,
):
    grps, tiles = dims
    devices = grps * tiles
    insts, comps, height, width = sens.shape
    ctrl, tile = rows_ref.shape
    tile_cols = width // tile
    half = (taps_ref.shape[0] - 1) // 2
    wide = 3 * tile
    low = LANES // ctrl
    high = ctrl // low
    slots = owner_ref.shape[1]
    ntiles = table_ref.shape[1]
    tile_pos = lax.axis_index("tile")
    me = lax.axis_index("grp") * tiles + tile_pos

    loads = [
        pltpu.make_async_copy(source, held, load_sems.at[n])
        for n, (source, held) in enumerate((
            (taps_hbm, taps_ref), (rows_hbm, rows_ref), (cols_hbm, cols_ref),
            (owner_hbm, owner_ref), (table_hbm, table_ref), (weight_hbm, weight),
            (sens_hbm, sens),
        ))
    ]
    for load in loads:
        load.start()

    barrier = pltpu.get_barrier_semaphore()

    def greet(step, carry):
        to = lax.rem(me + step, devices)
        pl.semaphore_signal(
            barrier, inc=1, device_id=(to // tiles, lax.rem(to, tiles)), device_id_type=MESH
        )
        return carry

    lax.fori_loop(1, devices, greet, 0)

    taps_wide[...] = jnp.zeros_like(taps_wide)
    col_op[...] = jnp.zeros_like(col_op)
    span = tile_cols * 3 * low
    lane = iota((ntiles, span), 1)
    y_of = lane // (3 * low)
    x_of = lax.rem(lane // low, 3) + tile_pos - 1
    wanted = (iota((ntiles, span), 0) == x_of * tile_cols + y_of) & (x_of >= 0) & (x_of < tiles)
    wanted_ref[...] = jnp.where(wanted, 1.0, 0.0).astype(BF16)
    copies = tile_cols * LANES
    from_row = iota((LANES, copies), 0)
    to_lane = iota((LANES, copies), 1)
    expand_ref[...] = jnp.where(
        (from_row // ctrl == to_lane // LANES) & (lax.rem(from_row, ctrl) == lax.rem(to_lane, ctrl)),
        1.0, 0.0,
    ).astype(BF16)
    keep = iota((low, LANES), 0) == iota((low, LANES), 1) // ctrl

    for load in loads[:3]:
        load.wait()
    taps_wide[:, : taps_ref.shape[0]] = taps_ref[...].astype(F32).reshape(1, -1)
    spread = jnp.broadcast_to(taps_wide[...], (tile, wide))
    band = pltpu.roll(spread, tile - half, 1, stride=1, stride_axis=0).astype(BF16)
    both = dot(jnp.concatenate([rows_ref[...], cols_ref[...]], axis=0), band).astype(BF16)
    row_op, piece = both[:ctrl], both[ctrl:]
    for y in range(tile_cols):
        first = max(y - 1, 0)
        last = min(y + 2, tile_cols)
        col_op[y * ctrl : (y + 1) * ctrl, first * tile : last * tile] = piece[
            :, (first - y + 1) * tile : (last - y + 1) * tile
        ]
    row_ops = jnp.concatenate(
        [row_op[:, d * tile : (d + 1) * tile] for d in (2, 1, 0)], axis=0
    )

    for load in loads[3:]:
        load.wait()
    owner_wide = jnp.broadcast_to(owner_ref[...].astype(F32), (slots, slots))
    owner = jnp.sum(
        jnp.where(iota((slots, slots), 0) == iota((slots, slots), 1), owner_wide, 0.0),
        axis=1, keepdims=True,
    )
    hit = jnp.where(owner == table_ref[...].astype(F32), 1.0, 0.0).astype(BF16)
    select = dot(hit, wanted_ref[...]).astype(BF16)

    field = sens[...].reshape(insts * comps * height, width)
    smooth = lax.dot_general(
        field, col_op[...], (((1,), (1,)), ((), ())), preferred_element_type=F32
    )
    block = comps * height
    total = weight[0] * smooth[:block]
    for i in range(1, insts):
        total = total + weight[i] * smooth[i * block : (i + 1) * block]
    total = total.astype(BF16)
    parts = jnp.concatenate(
        [dot(row_ops, total[k * height : (k + 1) * height]) for k in range(comps)], axis=0
    ).astype(BF16)
    grown = dot(parts, expand_ref[...])
    columns = []
    for k in range(comps):
        for h in range(high):
            pieces = []
            for y in range(tile_cols):
                for d in range(3):
                    at = (k * 3 + d) * ctrl + h * low
                    pieces.append(
                        jnp.where(keep, grown[at : at + low, y * LANES : (y + 1) * LANES], 0.0)
                    )
            columns.append(jnp.concatenate(pieces, axis=0))
    stacked = jnp.concatenate(columns, axis=1).astype(BF16)
    boxes = dot(select, stacked)
    for j in range(comps * high):
        msg[:, j, :] = boxes[:, j * LANES : (j + 1) * LANES]

    pl.semaphore_wait(barrier, devices - 1)

    def push(to, carry):
        @pl.when(to != me)
        def _():
            pltpu.make_async_remote_copy(
                src_ref=msg.at[to],
                dst_ref=recv.at[me],
                send_sem=send_sem,
                recv_sem=recv_sem,
                device_id=(to // tiles, lax.rem(to, tiles)),
                device_id_type=MESH,
            ).start()

        return carry

    lax.fori_loop(0, devices, push, 0)
    recv[me] = msg[me]
    others = recv.at[pl.ds(0, devices - 1)]
    pltpu.make_async_copy(others, others, recv_sem).wait()
    result = jnp.sum(recv[...], axis=0)
    for k in range(comps):
        for h in range(high):
            j = k * high + h
            out_ref[0, k : k + 1, h * LANES : (h + 1) * LANES] = result[j : j + 1]
    pltpu.make_async_copy(others, others, send_sem).wait()


def solution(mesh):
    grps, tiles = mesh.shape["grp"], mesh.shape["tile"]
    devices = grps * tiles

    def local(sens, weight, taps, rows, cols, table, owner):
        field = sens.transpose(0, 2, 1, 3)
        insts, comps, height, width = field.shape
        tile, ctrl = rows.shape
        slots = owner.shape[0]
        assert height == tile and slots == devices and LANES % ctrl == 0
        assert width // tile * ctrl == LANES and ctrl * ctrl % LANES == 0
        lines = comps * ctrl * ctrl // LANES
        return pl.pallas_call(
            functools.partial(kernel, (grps, tiles)),
            out_shape=jax.ShapeDtypeStruct((1, comps, ctrl * ctrl), F32),
            in_specs=[pl.BlockSpec(memory_space=pltpu.HBM)] * 7,
            out_specs=pl.BlockSpec(memory_space=pltpu.VMEM),
            scratch_shapes=[
                pltpu.VMEM((insts, comps, height, width), BF16),
                pltpu.SMEM(weight.shape, F32),
                pltpu.VMEM(taps.shape, BF16),
                pltpu.VMEM((ctrl, tile), BF16),
                pltpu.VMEM((ctrl, tile), BF16),
                pltpu.VMEM((1, table.shape[0]), jnp.int32),
                pltpu.VMEM((1, slots), jnp.int32),
                pltpu.VMEM((1, 3 * tile), F32),
                pltpu.VMEM((LANES, width), BF16),
                pltpu.VMEM((table.shape[0], width // tile * 3 * (LANES // ctrl)), BF16),
                pltpu.VMEM((LANES, width // tile * LANES), BF16),
                pltpu.VMEM((slots, lines, LANES), F32),
                pltpu.VMEM((devices, lines, LANES), F32),
                pltpu.SemaphoreType.DMA((7,)),
                pltpu.SemaphoreType.DMA,
                pltpu.SemaphoreType.DMA,
            ],
            compiler_params=pltpu.CompilerParams(
                collective_id=0, has_side_effects=True, vmem_limit_bytes=32 * 1024 * 1024
            ),
        )(
            *(
                pltpu.with_memory_space_constraint(operand, pltpu.HBM)
                for operand in (
                    field, weight, taps, rows.T, cols.T, table.reshape(1, -1), owner.reshape(1, -1)
                )
            )
        )

    placed = (P("grp", "tile", None, None), P("grp"), P(), P(), P(), P(), P())
    return jax.shard_map(
        local, mesh=mesh, in_specs=placed, out_specs=P(("grp", "tile"), None, None), check_vma=False
    )
```
